32 devices in a mesh: fsdp: 8 (over y, x, core), group: 4 (over z).
Axes of the slice: x: 2, y: 2, z: 4, core: 2. Of those that a mesh axis runs over, the one named last changes fastest.
Arguments:
- gradients: bfloat16 [32, 512, 512], P('group', 'fsdp'), may hold values from -6 to 6
- owners: int32 [4, 8], P('group'), may hold values from 0 to 7, each once within a row
- left_factors: float32 [32, 512, 512], P(('fsdp', 'group')), may hold values from -60 to 800, as said below
- right_factors: float32 [32, 512, 512], P(('fsdp', 'group')), may hold values from -60 to 800, as said below
- left_bases: float32 [32, 512, 512], P(('fsdp', 'group')), may hold values from -1 to 1
- right_bases: float32 [32, 512, 512], P(('fsdp', 'group')), may hold values from -1 to 1
- moments: float32 [32, 512, 512], P(('fsdp', 'group')), may hold values from 0.04 to 600
Outputs:
- updates: bfloat16 [32, 512, 512], P('group', 'fsdp')
The draws below stay inside these ranges and needn't reach their ends.
Inputs may be any that keep to these rules, and one draw needn't show every extreme that they name: Each row of owners is a permutation of the 8 indices along fsdp. `left_factors`: each block is symmetric and positive definite. `right_factors`: each block is symmetric and positive definite.
All inputs are finite; a program needn't handle non-finite values.
Results may differ from the reference program's by a relative error of at most 0.01.
Values may be sent and summed in bfloat16 or wider, within the bound.
A program may use at most 64 MiB of HBM per device.

```python
import jax
import jax.numpy as jnp
from jax import lax

B = 512
BLOCKS = 32
N_FSDP = 8
N_GROUP = 4


def definite(key):
    first_key, second_key = jax.random.split(key)
    level, bottom, top = (40.0, 0.5, 5.0)
    diagonal = jnp.exp(jax.random.uniform(first_key, (BLOCKS, B), jnp.float32, jnp.log(bottom), jnp.log(top)))
    random_rows = jax.random.normal(second_key, (BLOCKS, B, B), jnp.float32)

    def square(matrix):
        return jnp.dot(matrix, matrix.T, precision=lax.Precision.HIGHEST) / B
    crossed = lax.map(square, random_rows)
    return level * (crossed + diagonal[:, :, None] * jnp.eye(B, dtype=jnp.float32))


def orthonormal(key):
    random_rows = jax.random.normal(key, (BLOCKS, B, B), jnp.float32)
    basis_out, _ = jnp.linalg.qr(random_rows)
    return basis_out.astype(jnp.float32)


def draw_left_factors(key, part):
    return definite(jax.random.fold_in(key, 11))


def draw_right_factors(key, part):
    return definite(jax.random.fold_in(key, 12))


def draw_left_bases(key, part):
    return orthonormal(jax.random.fold_in(key, 13))


def draw_right_bases(key, part):
    return orthonormal(jax.random.fold_in(key, 14))


def draw_moments(key, part):
    row_key, column_key, entry_key = jax.random.split(jax.random.fold_in(key, 15), 3)
    level, spread = (0.1, 10.0)
    row_scale = jnp.exp(jax.random.uniform(row_key, (BLOCKS, B, 1), jnp.float32, 0.0, jnp.log(spread)))
    column_scale = jnp.exp(jax.random.uniform(column_key, (BLOCKS, 1, B), jnp.float32, 0.0, jnp.log(spread)))
    entries = jax.random.uniform(entry_key, (BLOCKS, B, B), jnp.float32, 0.5, 2.0)
    positions = jnp.arange(BLOCKS, dtype=jnp.float32)
    falling = 3.0 / (1.0 + 2.0 * positions / max(BLOCKS - 1, 1))
    return level * falling[:, None, None] * row_scale * column_scale * entries


def levels(stream_key, shape, shards, low, top_value):
    def one(axis_at, blocks):
        steps = jax.random.uniform(jax.random.fold_in(jax.random.fold_in(stream_key, 6), axis_at), (blocks,), jnp.float32, low / len(shards), top_value / len(shards))
        return jnp.repeat(jnp.exp(steps), shape[axis_at] // blocks).reshape((-1,) + (1,) * (len(shape) - axis_at - 1))

    loudness = one(*shards[0])
    for cut in shards[1:]:
        loudness = loudness * one(*cut)
    return loudness


def centred(stream_key, dims, deviation, most, cuts=(), kind=jnp.bfloat16):
    values = deviation * jax.random.normal(stream_key, dims, jnp.float32)
    if cuts:
        values = values * levels(stream_key, dims, cuts, -0.22, 0.18)
    return jnp.clip(values, -most, most).astype(kind)


def setup_inputs(seed: int = 0) -> dict:
    splits = jax.random.split(jax.random.key(seed), 8)
    gradients = centred(splits[0], (BLOCKS, B, B), 1.0, 6.0, ((0, 4), (1, 8)))
    owners = jax.vmap(lambda own: jax.random.permutation(own, N_FSDP))(jax.random.split(splits[1], N_GROUP)).reshape((N_GROUP, N_FSDP)).astype(jnp.int32)
    left_factors = draw_left_factors(jax.random.fold_in(splits[7], 71), 0)
    right_factors = draw_right_factors(jax.random.fold_in(splits[7], 71), 0)
    left_bases = draw_left_bases(jax.random.fold_in(splits[7], 71), 0)
    right_bases = draw_right_bases(jax.random.fold_in(splits[7], 71), 0)
    moments = draw_moments(jax.random.fold_in(splits[7], 71), 0)
    return dict(gradients=gradients, owners=owners, left_factors=left_factors, right_factors=right_factors, left_bases=left_bases, right_bases=right_bases, moments=moments)


factor_decay = 0.95
moment_decay = 0.95
epsilon = 1e-08
clip_rms = 0.25

def refresh(factor, old_basis):
    projected = jnp.dot(factor, old_basis, precision=lax.Precision.HIGHEST)
    correlation = jnp.dot(projected.T, projected, precision=lax.Precision.HIGHEST)
    cholesky_factor = jnp.linalg.cholesky(correlation)
    solved = jax.scipy.linalg.solve_triangular(cholesky_factor, projected.T, lower=True)
    return solved.T.astype(jnp.bfloat16)

def precondition(gradient, left_old, right_old, left_basis, right_basis, moment):
    left_gram = jnp.dot(gradient.astype(jnp.float32), gradient.T.astype(jnp.float32), preferred_element_type=jnp.float32)
    right_gram = jnp.dot(gradient.T.astype(jnp.float32), gradient.astype(jnp.float32), preferred_element_type=jnp.float32)
    left_new = factor_decay * left_old + (1.0 - factor_decay) * left_gram
    right_new = factor_decay * right_old + (1.0 - factor_decay) * right_gram
    left_rotate = refresh(left_new, left_basis)
    right_rotate = refresh(right_new, right_basis)
    first = jnp.dot(left_rotate.T.astype(jnp.float32), gradient.astype(jnp.float32), preferred_element_type=jnp.float32).astype(jnp.bfloat16)
    rotated = jnp.dot(first.astype(jnp.float32), right_rotate.astype(jnp.float32), preferred_element_type=jnp.float32)
    moment_new = moment_decay * moment + (1.0 - moment_decay) * rotated * rotated
    normed = (rotated / (jnp.sqrt(moment_new) + epsilon)).astype(jnp.bfloat16)
    back = jnp.dot(left_rotate.astype(jnp.float32), normed.astype(jnp.float32), preferred_element_type=jnp.float32).astype(jnp.bfloat16)
    return jnp.dot(back.astype(jnp.float32), right_rotate.T.astype(jnp.float32), preferred_element_type=jnp.float32)

def reference(gradients, owners, left_factors, right_factors, left_bases, right_bases, moments):
    slot_table = owners.astype(jnp.int32) * N_GROUP + jnp.arange(N_GROUP, dtype=jnp.int32)[:, None]
    slot_list = slot_table.reshape(-1).astype(jnp.int32)

    def single(pair):
        gradient, slot = pair

        def pick(states):
            return lax.dynamic_index_in_dim(states, slot, 0, keepdims=False)
        return precondition(gradient, pick(left_factors), pick(right_factors), pick(left_bases), pick(right_bases), pick(moments))
    unclipped = lax.map(single, (gradients, slot_list))
    total = jnp.sum(unclipped * unclipped)
    count = jnp.asarray(BLOCKS * B * B, jnp.float32)
    scale = jnp.minimum(1.0, clip_rms * jnp.sqrt(count) / jnp.sqrt(total + 1e-06))
    return (scale * unclipped).astype(jnp.bfloat16)
```

```python
import functools

import jax
import jax.numpy as jnp
from jax import lax
from jax.experimental import pallas as pl
from jax.experimental.pallas import tpu as pltpu
from jax.sharding import PartitionSpec as P

factor_decay = 0.95
moment_decay = 0.95
epsilon = 1e-08
clip_rms = 0.25

panel = 128
tile = 8
NN = (((1,), (0,)), ((), ()))
NT = (((1,), (1,)), ((), ()))
TN = (((0,), (0,)), ((), ()))


def mm(a, b, dims):
    return lax.dot_general(a, b, dims, preferred_element_type=jnp.float32)


def split(x):
    high = x.astype(jnp.bfloat16)
    low = (x - high.astype(jnp.float32)).astype(jnp.bfloat16)
    return high, low


def mm3(a, b, dims):
    (ah, al), (bh, bl) = a, b
    return mm(ah, bh, dims) + (mm(ah, bl, dims) + mm(al, bh, dims))


def gram(x):
    return lax.dot_general(
        x, x, NT, precision=lax.Precision.HIGHEST, preferred_element_type=jnp.float32
    )


def lane_copy(x, at):
    return jnp.broadcast_to(x[:, at : at + 1], x.shape)


def row_copy(x, at):
    return jnp.broadcast_to(x[at : at + 1, :], x.shape)


def reciprocal(x):
    guess = pl.reciprocal(x, approx=True)
    guess = guess * (2.0 - x * guess)
    return guess * (2.0 - x * guess)


def root_reciprocal(x):
    guess = lax.rsqrt(x)
    return guess * (1.5 - 0.5 * x * guess * guess)


def pivot_rows(first, own, columns):
    row_id = lax.broadcasted_iota(jnp.int32, own.shape, 0)
    lane_id = lax.broadcasted_iota(jnp.int32, own.shape, 1) - first
    inside = (lane_id >= 0) & (lane_id < tile)
    solved = jnp.where(inside, jnp.where(lane_id == row_id, 1.0, 0.0), own)
    factored = solved
    columns = list(columns)
    for j in range(0, tile, 2):
        left, right = columns[j], columns[j + 1]
        a, b, c = row_copy(left, j), row_copy(left, j + 1), row_copy(right, j + 1)
        det = a * c - b * b
        inv = reciprocal(det)
        ia, ib, ic = c * inv, b * inv, a * inv
        root = root_reciprocal(a)
        tail = root_reciprocal(det * root * root)
        is_first, is_second = row_id == j, row_id == j + 1

        def eliminate(x):
            upper, lower = row_copy(x, j), row_copy(x, j + 1)
            new_upper = ia * upper - ib * lower
            new_lower = ic * lower - ib * upper
            rest = x - left * new_upper - right * new_lower
            new = jnp.where(is_first, new_upper, jnp.where(is_second, new_lower, rest))
            return new, upper, lower

        for l in range(j + 2, tile):
            columns[l] = eliminate(columns[l])[0]
        solved, upper, lower = eliminate(solved)
        y_upper = upper * root
        y_lower = (lower - b * root * y_upper) * tail
        factored = jnp.where(is_first, y_upper, jnp.where(is_second, y_lower, factored))
    return solved, factored


def inverse_cholesky(matrices):
    count = panel // tile
    rows = [[m[g * tile : (g + 1) * tile, :] for g in range(count)] for m in matrices]
    done = [[None] * count for _ in matrices]
    lane_id = lax.broadcasted_iota(jnp.int32, (tile, panel), 1)
    for p in range(count):
        first = p * tile
        inside = (lane_id >= first) & (lane_id < first + tile)
        for m, groups in enumerate(rows):
            columns = [lane_copy(groups[p], first + j) for j in range(tile)]
            solved, factored = pivot_rows(first, groups[p], columns)
            done[m][p] = jnp.where(lane_id < first + tile, factored, 0.0)
            if p + 1 < count:
                solved_rows = [row_copy(solved, j) for j in range(tile)]
                for g in range(p + 1, count):
                    old = groups[g]
                    new = jnp.where(inside, 0.0, old)
                    for j in range(tile):
                        new = new - lane_copy(old, first + j) * solved_rows[j]
                    groups[g] = new
    return [jnp.concatenate(d, axis=0) for d in done]


def refresh(projected, high, low, panels):
    for side in range(2):
        high[side] = jnp.zeros_like(high[side])
        low[side] = jnp.zeros_like(low[side])

    def step(k, carry):
        rows = pl.ds(pl.multiple_of(k * panel, panel), panel)
        blocks = []
        for side in range(2):
            block = projected[side, rows, :]
            basis = (high[side], low[side])
            inner = mm3(split(block), basis, NT)
            block = block - mm3(split(inner), basis, NN)
            block = block * lax.rsqrt(jnp.sum(block * block, axis=1, keepdims=True))
            blocks.append(block)
        inverses = inverse_cholesky([gram(b) for b in blocks])
        for side in range(2):
            q = mm3(split(inverses[side]), split(blocks[side]), NN)
            qh, ql = split(q)
            high[side, rows, :] = qh
            low[side, rows, :] = ql
        return carry

    lax.fori_loop(0, panels, step, 0)


def local_kernel(
    g_ref, l_ref, r_ref, ql_ref, qr_ref, v_ref, u_ref, s_ref, projected, high, low
):
    width = g_ref.shape[0]
    g = g_ref[...]
    left = factor_decay * l_ref[0] + (1.0 - factor_decay) * mm(g, g, NT)
    projected[0] = mm3(split(ql_ref[0]), split(left), TN)
    right = factor_decay * r_ref[0] + (1.0 - factor_decay) * mm(g, g, TN)
    projected[1] = mm3(split(qr_ref[0]), split(right), TN)
    refresh(projected, high, low, width // panel)
    first = mm(high[0], g, NN).astype(jnp.bfloat16)
    rotated = mm(first, high[1], NT)
    moment = moment_decay * v_ref[0] + (1.0 - moment_decay) * rotated * rotated
    normed = (rotated / (jnp.sqrt(moment) + epsilon)).astype(jnp.bfloat16)
    back = mm(high[0], normed, TN).astype(jnp.bfloat16)
    update = mm(back, high[1], NN)
    u_ref[...] = update.astype(jnp.bfloat16)
    s_ref[...] = jnp.sum(update * update, axis=0, keepdims=True)


def local(gradient, *states):
    width = gradient.shape[0]
    vmem = pl.BlockSpec(memory_space=pltpu.VMEM)
    return pl.pallas_call(
        local_kernel,
        out_shape=(
            jax.ShapeDtypeStruct((width, width), jnp.bfloat16),
            jax.ShapeDtypeStruct((1, width), jnp.float32),
        ),
        in_specs=[vmem] * 6,
        out_specs=(vmem, vmem),
        scratch_shapes=[
            pltpu.VMEM((2, width, width), jnp.float32),
            pltpu.VMEM((2, width, width), jnp.bfloat16),
            pltpu.VMEM((2, width, width), jnp.bfloat16),
        ],
        compiler_params=pltpu.CompilerParams(vmem_limit_bytes=48 * 1024 * 1024),
        name="local_update",
    )(gradient, *states)


def on_device(gradients, owners, left_factors, right_factors, left_bases, right_bases, moments):
    fsdp_count = lax.axis_size("fsdp")
    owner_row = owners[0]
    positions = jnp.arange(fsdp_count, dtype=jnp.int32)
    matches = owner_row[:, None] == positions[None, :]
    inverse = jnp.sum(jnp.where(matches, positions[:, None], 0), axis=0)
    outgoing = jnp.take(gradients, inverse, axis=0)
    gathered = lax.all_to_all(outgoing, "fsdp", split_axis=0, concat_axis=1, tiled=True)
    gradient = gathered[0]
    width = gradient.shape[0]
    unclipped, sums = local(
        gradient, left_factors, right_factors, left_bases, right_bases, moments
    )
    squares = jnp.sum(sums)
    count = jnp.asarray(fsdp_count * lax.axis_size("group") * width * width, jnp.float32)
    pieces = lax.all_to_all(
        unclipped[None], "fsdp", split_axis=1, concat_axis=0, tiled=True
    ).astype(jnp.float32)
    total = lax.psum(squares, ("fsdp", "group"))
    scale = jnp.minimum(1.0, clip_rms * jnp.sqrt(count) / jnp.sqrt(total + 1e-06))
    return (scale * jnp.take(pieces, owner_row, axis=0)).astype(jnp.bfloat16)


def solution(mesh):
    in_specs = (
        P("group", "fsdp", None),
        P("group", None),
        P(("fsdp", "group"), None, None),
        P(("fsdp", "group"), None, None),
        P(("fsdp", "group"), None, None),
        P(("fsdp", "group"), None, None),
        P(("fsdp", "group"), None, None),
    )
    out_specs = P("group", "fsdp", None)
    return jax.shard_map(
        on_device, mesh=mesh, in_specs=in_specs, out_specs=out_specs, check_vma=False
    )
```

```python
import functools

import jax
import jax.numpy as jnp
from jax import lax
from jax.experimental import pallas as pl
from jax.experimental.pallas import tpu as pltpu
from jax.sharding import PartitionSpec as P

factor_decay = 0.95
moment_decay = 0.95
epsilon = 1e-08
clip_rms = 0.25

panel = 128
tile = 8
NN = (((1,), (0,)), ((), ()))
NT = (((1,), (1,)), ((), ()))
TN = (((0,), (0,)), ((), ()))


def mm(a, b, dims):
    return lax.dot_general(a, b, dims, preferred_element_type=jnp.float32)


def split(x):
    high = x.astype(jnp.bfloat16)
    low = (x - high.astype(jnp.float32)).astype(jnp.bfloat16)
    return high, low


def mm3(a, b, dims):
    (ah, al), (bh, bl) = a, b
    return mm(ah, bh, dims) + (mm(ah, bl, dims) + mm(al, bh, dims))


def gram(x):
    return lax.dot_general(
        x, x, NT, precision=lax.Precision.HIGHEST, preferred_element_type=jnp.float32
    )


def lane_copy(x, at):
    return jnp.broadcast_to(x[:, at : at + 1], x.shape)


def row_copy(x, at):
    return jnp.broadcast_to(x[at : at + 1, :], x.shape)


def reciprocal(x):
    guess = pl.reciprocal(x, approx=True)
    return guess * (2.0 - x * guess)


def root_reciprocal(x):
    guess = lax.rsqrt(x)
    return guess * (1.5 - 0.5 * x * guess * guess)


def pivot_rows(first, own, columns):
    row_id = lax.broadcasted_iota(jnp.int32, own.shape, 0)
    lane_id = lax.broadcasted_iota(jnp.int32, own.shape, 1) - first
    inside = (lane_id >= 0) & (lane_id < tile)
    solved = jnp.where(inside, jnp.where(lane_id == row_id, 1.0, 0.0), own)
    factored = solved
    columns = list(columns)
    for j in range(0, tile, 2):
        left, right = columns[j], columns[j + 1]
        a, b, c = row_copy(left, j), row_copy(left, j + 1), row_copy(right, j + 1)
        det = a * c - b * b
        inv = reciprocal(det)
        ia, ib, ic = c * inv, b * inv, a * inv
        root = root_reciprocal(a)
        tail = root_reciprocal(det * root * root)
        is_first, is_second = row_id == j, row_id == j + 1

        def eliminate(x):
            upper, lower = row_copy(x, j), row_copy(x, j + 1)
            new_upper = ia * upper - ib * lower
            new_lower = ic * lower - ib * upper
            rest = x - left * new_upper - right * new_lower
            new = jnp.where(is_first, new_upper, jnp.where(is_second, new_lower, rest))
            return new, upper, lower

        for l in range(j + 2, tile):
            columns[l] = eliminate(columns[l])[0]
        solved, upper, lower = eliminate(solved)
        y_upper = upper * root
        y_lower = (lower - b * root * y_upper) * tail
        factored = jnp.where(is_first, y_upper, jnp.where(is_second, y_lower, factored))
    return solved, factored


def inverse_cholesky(matrices):
    count = panel // tile
    rows = [[m[g * tile : (g + 1) * tile, :] for g in range(count)] for m in matrices]
    done = [[None] * count for _ in matrices]
    lane_id = lax.broadcasted_iota(jnp.int32, (tile, panel), 1)
    for p in range(count):
        first = p * tile
        inside = (lane_id >= first) & (lane_id < first + tile)
        for m, groups in enumerate(rows):
            columns = [lane_copy(groups[p], first + j) for j in range(tile)]
            solved, factored = pivot_rows(first, groups[p], columns)
            done[m][p] = jnp.where(lane_id < first + tile, factored, 0.0)
            if p + 1 < count:
                solved_rows = [row_copy(solved, j) for j in range(tile)]
                for g in range(p + 1, count):
                    old = groups[g]
                    terms = [lane_copy(old, first + j) * solved_rows[j] for j in range(tile)]
                    while len(terms) > 1:
                        terms = [x + y for x, y in zip(terms[::2], terms[1::2])]
                    groups[g] = jnp.where(inside, 0.0, old) - terms[0]
    return [jnp.concatenate(d, axis=0) for d in done]


def project_out(side, first, projected, basis_high, basis_low):
    rest = projected[side, first:, :]
    rest_high, rest_low = split(rest)
    both = jnp.concatenate([basis_high, basis_low], axis=0)
    wide = mm(rest_high, both, NT)
    inner = wide[:, :panel] + (wide[:, panel:] + mm(rest_low, basis_high, NT))
    inner_high, inner_low = split(inner)
    twice = jnp.concatenate([basis_high, basis_high], axis=0)
    split_inner = jnp.concatenate([inner_high, inner_low], axis=1)
    part = mm(split_inner, twice, NN) + mm(inner_high, basis_low, NN)
    projected[side, first:, :] = rest - part


def refresh(projected, high, low, panels):
    def step(k, carry):
        rows = pl.ds(pl.multiple_of(k * panel, panel), panel)
        blocks = []
        for side in range(2):
            block = projected[side, rows, :]
            block = block * lax.rsqrt(jnp.sum(block * block, axis=1, keepdims=True))
            blocks.append(block)
        inverses = inverse_cholesky([gram(b) for b in blocks])
        for side in range(2):
            q = mm3(split(inverses[side]), split(blocks[side]), NN)
            qh, ql = split(q)
            high[side, rows, :] = qh
            low[side] = ql
        for at in range(panels - 1):

            @pl.when(k == at)
            def _():
                for side in range(2):
                    own = high[side, at * panel : (at + 1) * panel, :]
                    project_out(side, (at + 1) * panel, projected, own, low[side])

        return carry

    lax.fori_loop(0, panels, step, 0)


def local_kernel(
    g_ref, l_ref, r_ref, ql_ref, qr_ref, v_ref, u_ref, s_ref, projected, high, low
):
    width = g_ref.shape[0]
    g = g_ref[...]
    left = factor_decay * l_ref[0] + (1.0 - factor_decay) * mm(g, g, NT)
    projected[0] = mm3(split(ql_ref[0]), split(left), TN)
    right = factor_decay * r_ref[0] + (1.0 - factor_decay) * mm(g, g, TN)
    projected[1] = mm3(split(qr_ref[0]), split(right), TN)
    refresh(projected, high, low, width // panel)
    first = mm(high[0], g, NN).astype(jnp.bfloat16)
    rotated = mm(first, high[1], NT)
    moment = moment_decay * v_ref[0] + (1.0 - moment_decay) * rotated * rotated
    normed = (rotated / (jnp.sqrt(moment) + epsilon)).astype(jnp.bfloat16)
    back = mm(high[0], normed, TN).astype(jnp.bfloat16)
    update = mm(back, high[1], NN)
    u_ref[...] = update.astype(jnp.bfloat16)
    squares = jnp.sum((update * update).reshape(width // 8, 8, width), axis=0)
    s_ref[...] = sum(squares[:, at : at + 128] for at in range(0, width, 128))


def local(gradient, *states):
    width = gradient.shape[0]
    vmem = pl.BlockSpec(memory_space=pltpu.VMEM)
    return pl.pallas_call(
        local_kernel,
        out_shape=(
            jax.ShapeDtypeStruct((width, width), jnp.bfloat16),
            jax.ShapeDtypeStruct((8, 128), jnp.float32),
        ),
        in_specs=[vmem] * 6,
        out_specs=(vmem, vmem),
        scratch_shapes=[
            pltpu.VMEM((2, width, width), jnp.float32),
            pltpu.VMEM((2, width, width), jnp.bfloat16),
            pltpu.VMEM((2, panel, width), jnp.bfloat16),
        ],
        compiler_params=pltpu.CompilerParams(vmem_limit_bytes=48 * 1024 * 1024),
        name="local_update",
    )(gradient, *states)


def position(owners_ref, owner, count):
    at = 0
    for j in range(1, count):
        at = jnp.where(owners_ref[0, j] == owner, j, at)
    return at


def meet(axes):
    barrier = pltpu.get_barrier_semaphore()
    others = 0
    for axis, count in axes:
        me = lax.axis_index(axis)
        for d in range(1, count):
            pl.semaphore_signal(
                barrier,
                inc=1,
                device_id={axis: lax.rem(me + d, count)},
                device_id_type=pl.DeviceIdType.MESH,
            )
            others += 1
    pl.semaphore_wait(barrier, others)


def send(source, target, send_sem, recv_sem, axis, to):
    copy = pltpu.make_async_remote_copy(
        src_ref=source,
        dst_ref=target,
        send_sem=send_sem,
        recv_sem=recv_sem,
        device_id={axis: to},
        device_id_type=pl.DeviceIdType.MESH,
    )
    copy.start()
    return copy


def collect_kernel(count, owners_ref, g_ref, out_ref, outgoing, landing, send_sem, recv_sem):
    me = lax.axis_index("fsdp")
    height = g_ref.shape[1]
    for d in range(1, count):
        outgoing[d] = g_ref[position(owners_ref, lax.rem(me + d, count), count)]
    meet([("fsdp", count)])
    copies = []
    for d in range(1, count):
        to = lax.rem(me + d, count)
        copies.append(
            send(outgoing.at[d], landing.at[me], send_sem.at[d], recv_sem.at[d], "fsdp", to)
        )
    landing[me] = g_ref[position(owners_ref, me, count)]
    for copy in copies:
        copy.wait()
    for f in range(count):
        out_ref[f * height : (f + 1) * height, :] = landing[f]


def collect(owners, gradients, count):
    _, height, width = gradients.shape
    return pl.pallas_call(
        functools.partial(collect_kernel, count),
        out_shape=jax.ShapeDtypeStruct((count * height, width), gradients.dtype),
        in_specs=[
            pl.BlockSpec(memory_space=pltpu.SMEM),
            pl.BlockSpec(memory_space=pltpu.VMEM),
        ],
        out_specs=pl.BlockSpec(memory_space=pltpu.VMEM),
        scratch_shapes=[
            pltpu.VMEM((count, height, width), gradients.dtype),
            pltpu.VMEM((count, height, width), gradients.dtype),
            pltpu.SemaphoreType.DMA((count,)),
            pltpu.SemaphoreType.DMA((count,)),
        ],
        compiler_params=pltpu.CompilerParams(
            collective_id=0, has_side_effects=True, vmem_limit_bytes=16 * 1024 * 1024
        ),
        name="collect_gradient",
    )(owners, gradients)


def spread_kernel(
    count,
    groups,
    owners_ref,
    u_ref,
    s_ref,
    out_ref,
    pieces,
    near,
    far,
    mine,
    piece_send,
    piece_recv,
    near_send,
    near_recv,
    far_send,
    far_recv,
):
    me, group = lax.axis_index("fsdp"), lax.axis_index("group")
    height = out_ref.shape[1]
    meet([("fsdp", count), ("group", groups)])
    near_copies, piece_copies, far_copies = [], [], []
    for d in range(1, count):
        to = lax.rem(me + d, count)
        near_copies.append(
            send(s_ref, near.at[me], near_send.at[d], near_recv.at[d], "fsdp", to)
        )
    for d in range(1, count):
        to = lax.rem(me + d, count)
        rows = pl.ds(pl.multiple_of(to * height, height), height)
        piece_copies.append(
            send(u_ref.at[rows], pieces.at[me], piece_send.at[d], piece_recv.at[d], "fsdp", to)
        )
    near[me] = s_ref[...]
    pieces[me] = u_ref[pl.ds(pl.multiple_of(me * height, height), height), :]
    for copy in near_copies:
        copy.wait()
    mine[...] = sum(near[f] for f in range(count))
    for d in range(1, groups):
        to = lax.rem(group + d, groups)
        far_copies.append(
            send(mine, far.at[group], far_send.at[d], far_recv.at[d], "group", to)
        )
    far[group] = mine[...]
    for copy in far_copies:
        copy.wait()
    total = jnp.sum(sum(far[g] for g in range(groups)), axis=1, keepdims=True)
    total = jnp.sum(total, axis=0, keepdims=True)
    entries = count * groups * u_ref.shape[0] * u_ref.shape[1]
    ceiling = clip_rms * entries**0.5
    scale = jnp.minimum(1.0, ceiling / jnp.sqrt(total + 1e-06))
    for copy in piece_copies:
        copy.wait()
    for j in range(count):
        piece = pieces[owners_ref[0, j]].astype(jnp.float32)
        out_ref[j] = (scale * piece).astype(out_ref.dtype)


def spread(owners, update, squares, count, groups):
    width = update.shape[1]
    height = update.shape[0] // count
    vmem = pl.BlockSpec(memory_space=pltpu.VMEM)
    semaphores = pltpu.SemaphoreType.DMA
    return pl.pallas_call(
        functools.partial(spread_kernel, count, groups),
        out_shape=jax.ShapeDtypeStruct((count, height, width), update.dtype),
        in_specs=[pl.BlockSpec(memory_space=pltpu.SMEM), vmem, vmem],
        out_specs=vmem,
        scratch_shapes=[
            pltpu.VMEM((count, height, width), update.dtype),
            pltpu.VMEM((count, 8, 128), jnp.float32),
            pltpu.VMEM((groups, 8, 128), jnp.float32),
            pltpu.VMEM((8, 128), jnp.float32),
            semaphores((count,)),
            semaphores((count,)),
            semaphores((count,)),
            semaphores((count,)),
            semaphores((groups,)),
            semaphores((groups,)),
        ],
        compiler_params=pltpu.CompilerParams(
            collective_id=1, has_side_effects=True, vmem_limit_bytes=16 * 1024 * 1024
        ),
        name="spread_update",
    )(owners, update, squares)


def on_device(gradients, owners, left_factors, right_factors, left_bases, right_bases, moments):
    count, groups = lax.axis_size("fsdp"), lax.axis_size("group")
    gradient = collect(owners, gradients, count)
    update, squares = local(
        gradient, left_factors, right_factors, left_bases, right_bases, moments
    )
    return spread(owners, update, squares, count, groups)


def solution(mesh):
    in_specs = (
        P("group", "fsdp", None),
        P("group", None),
        P(("fsdp", "group"), None, None),
        P(("fsdp", "group"), None, None),
        P(("fsdp", "group"), None, None),
        P(("fsdp", "group"), None, None),
        P(("fsdp", "group"), None, None),
    )
    out_specs = P("group", "fsdp", None)
    return jax.shard_map(
        on_device, mesh=mesh, in_specs=in_specs, out_specs=out_specs, check_vma=False
    )
```

```python
import functools

import jax
import jax.numpy as jnp
from jax import lax
from jax.experimental import pallas as pl
from jax.experimental.pallas import tpu as pltpu
from jax.sharding import PartitionSpec as P

factor_decay = 0.95
moment_decay = 0.95
epsilon = 1e-08
clip_rms = 0.25

panel = 128
tile = 8
NN = (((1,), (0,)), ((), ()))
NT = (((1,), (1,)), ((), ()))
TN = (((0,), (0,)), ((), ()))


def mm(a, b, dims):
    return lax.dot_general(a, b, dims, preferred_element_type=jnp.float32)


def split(x):
    high = x.astype(jnp.bfloat16)
    low = (x - high.astype(jnp.float32)).astype(jnp.bfloat16)
    return high, low


def mm3(a, b, dims):
    (ah, al), (bh, bl) = a, b
    return mm(ah, bh, dims) + (mm(ah, bl, dims) + mm(al, bh, dims))


def gram(x):
    return lax.dot_general(
        x, x, NT, precision=lax.Precision.HIGHEST, preferred_element_type=jnp.float32
    )


def lane_copy(x, at):
    return jnp.broadcast_to(x[:, at : at + 1], x.shape)


def row_copy(x, at):
    return jnp.broadcast_to(x[at : at + 1, :], x.shape)


def root_reciprocal(x):
    guess = lax.rsqrt(x)
    return guess * (1.5 - 0.5 * x * guess * guess)


def pivot_rows(first, own, columns):
    row_id = lax.broadcasted_iota(jnp.int32, own.shape, 0)
    lane_id = lax.broadcasted_iota(jnp.int32, own.shape, 1) - first
    inside = (lane_id >= 0) & (lane_id < tile)
    solved = jnp.where(inside, jnp.where(lane_id == row_id, 1.0, 0.0), own)
    factored = solved
    columns = list(columns)
    for j in range(0, tile, 2):
        left, right = columns[j], columns[j + 1]
        a, b, c = row_copy(left, j), row_copy(left, j + 1), row_copy(right, j + 1)
        det = a * c - b * b
        inv = pl.reciprocal(det, approx=True)
        root = root_reciprocal(a)
        tail = root_reciprocal(det * root * root)
        is_first, is_second = row_id == j, row_id == j + 1
        left = left - jnp.where(is_first, 1.0, 0.0)
        right = right - jnp.where(is_second, 1.0, 0.0)

        def eliminate(x):
            upper, lower = row_copy(x, j), row_copy(x, j + 1)
            part = left * (c * upper - b * lower) + right * (a * lower - b * upper)
            return x - part * inv, upper, lower

        for l in range(j + 2, tile):
            columns[l] = eliminate(columns[l])[0]
        solved, upper, lower = eliminate(solved)
        y_upper = upper * root
        y_lower = (lower - b * root * y_upper) * tail
        factored = jnp.where(is_first, y_upper, jnp.where(is_second, y_lower, factored))
    return solved, factored


def inverse_cholesky(matrices):
    count = panel // tile
    rows = [[m[g * tile : (g + 1) * tile, :] for g in range(count)] for m in matrices]
    done = [[None] * count for _ in matrices]
    lane_id = lax.broadcasted_iota(jnp.int32, (tile, panel), 1)
    for p in range(count):
        first = p * tile
        inside = (lane_id >= first) & (lane_id < first + tile)
        for m, groups in enumerate(rows):
            columns = [lane_copy(groups[p], first + j) for j in range(tile)]
            solved, factored = pivot_rows(first, groups[p], columns)
            done[m][p] = jnp.where(lane_id < first + tile, factored, 0.0)
            if p + 1 < count:
                solved_rows = [row_copy(solved, j) for j in range(tile)]
                for g in range(p + 1, count):
                    old = groups[g]
                    terms = [lane_copy(old, first + j) * solved_rows[j] for j in range(tile)]
                    while len(terms) > 1:
                        terms = [x + y for x, y in zip(terms[::2], terms[1::2])]
                    groups[g] = jnp.where(inside, 0.0, old) - terms[0]
    return [jnp.concatenate(d, axis=0) for d in done]


def project_out(side, first, projected, basis_high, basis_low):
    rest = projected[side, first:, :]
    rest_high, rest_low = split(rest)
    both = jnp.concatenate([basis_high, basis_low], axis=0)
    wide = mm(rest_high, both, NT)
    inner = wide[:, :panel] + (wide[:, panel:] + mm(rest_low, basis_high, NT))
    inner_high, inner_low = split(inner)
    twice = jnp.concatenate([basis_high, basis_high], axis=0)
    split_inner = jnp.concatenate([inner_high, inner_low], axis=1)
    part = mm(split_inner, twice, NN) + mm(inner_high, basis_low, NN)
    projected[side, first:, :] = rest - part


def refresh(projected, high, low, panels):
    def step(k, carry):
        rows = pl.ds(pl.multiple_of(k * panel, panel), panel)
        blocks = []
        for side in range(2):
            block = projected[side, rows, :]
            block = block * lax.rsqrt(jnp.sum(block * block, axis=1, keepdims=True))
            blocks.append(block)
        inverses = inverse_cholesky([gram(b) for b in blocks])
        for side in range(2):
            q = mm3(split(inverses[side]), split(blocks[side]), NN)
            qh, ql = split(q)
            high[side, rows, :] = qh
            low[side] = ql
        for at in range(panels - 1):

            @pl.when(k == at)
            def _():
                for side in range(2):
                    own = high[side, at * panel : (at + 1) * panel, :]
                    project_out(side, (at + 1) * panel, projected, own, low[side])

        return carry

    lax.fori_loop(0, panels, step, 0)


def local_kernel(
    g_ref, l_ref, r_ref, ql_ref, qr_ref, v_ref, u_ref, s_ref, projected, high, low
):
    width = g_ref.shape[0]
    g = g_ref[...]
    left = factor_decay * l_ref[0] + (1.0 - factor_decay) * mm(g, g, NT)
    projected[0] = mm3(split(ql_ref[0]), split(left), TN)
    right = factor_decay * r_ref[0] + (1.0 - factor_decay) * mm(g, g, TN)
    projected[1] = mm3(split(qr_ref[0]), split(right), TN)
    refresh(projected, high, low, width // panel)
    first = mm(high[0], g, NN).astype(jnp.bfloat16)
    rotated = mm(first, high[1], NT)
    moment = moment_decay * v_ref[0] + (1.0 - moment_decay) * rotated * rotated
    normed = (rotated / (jnp.sqrt(moment) + epsilon)).astype(jnp.bfloat16)
    back = mm(high[0], normed, TN).astype(jnp.bfloat16)
    update = mm(back, high[1], NN)
    u_ref[...] = update.astype(jnp.bfloat16)
    squares = jnp.sum((update * update).reshape(width // 8, 8, width), axis=0)
    s_ref[...] = sum(squares[:, at : at + 128] for at in range(0, width, 128))


def local(gradient, *states):
    width = gradient.shape[0]
    flat = pl.BlockSpec((width, width), lambda i: (0, 0))
    state = pl.BlockSpec((1, width, width), lambda i: (0, 0, 0))
    return pl.pallas_call(
        local_kernel,
        grid=(1,),
        out_shape=(
            jax.ShapeDtypeStruct((width, width), jnp.bfloat16),
            jax.ShapeDtypeStruct((8, 128), jnp.float32),
        ),
        in_specs=[flat] + [state] * 5,
        out_specs=(flat, pl.BlockSpec((8, 128), lambda i: (0, 0))),
        scratch_shapes=[
            pltpu.VMEM((2, width, width), jnp.float32),
            pltpu.VMEM((2, width, width), jnp.bfloat16),
            pltpu.VMEM((2, panel, width), jnp.bfloat16),
        ],
        compiler_params=pltpu.CompilerParams(vmem_limit_bytes=48 * 1024 * 1024),
        name="local_update",
    )(gradient, *states)


def position(owners_ref, owner, count):
    at = 0
    for j in range(1, count):
        at = jnp.where(owners_ref[0, j] == owner, j, at)
    return at


def meet(axes):
    barrier = pltpu.get_barrier_semaphore()
    others = 0
    for axis, count in axes:
        me = lax.axis_index(axis)
        for d in range(1, count):
            pl.semaphore_signal(
                barrier,
                inc=1,
                device_id={axis: lax.rem(me + d, count)},
                device_id_type=pl.DeviceIdType.MESH,
            )
            others += 1
    pl.semaphore_wait(barrier, others)


def send(source, target, send_sem, recv_sem, axis, to):
    copy = pltpu.make_async_remote_copy(
        src_ref=source,
        dst_ref=target,
        send_sem=send_sem,
        recv_sem=recv_sem,
        device_id={axis: to},
        device_id_type=pl.DeviceIdType.MESH,
    )
    copy.start()
    return copy


def collect_kernel(count, owners_ref, g_ref, out_ref, outgoing, landing, send_sem, recv_sem):
    me = lax.axis_index("fsdp")
    height = g_ref.shape[1]
    for d in range(1, count):
        outgoing[d] = g_ref[position(owners_ref, lax.rem(me + d, count), count)]
    meet([("fsdp", count)])
    copies = []
    for d in range(1, count):
        to = lax.rem(me + d, count)
        copies.append(
            send(outgoing.at[d], landing.at[me], send_sem.at[d], recv_sem.at[d], "fsdp", to)
        )
    landing[me] = g_ref[position(owners_ref, me, count)]
    for copy in copies:
        copy.wait()
    for f in range(count):
        out_ref[f * height : (f + 1) * height, :] = landing[f]


def collect(owners, gradients, count):
    _, height, width = gradients.shape
    return pl.pallas_call(
        functools.partial(collect_kernel, count),
        out_shape=jax.ShapeDtypeStruct((count * height, width), gradients.dtype),
        in_specs=[
            pl.BlockSpec(memory_space=pltpu.SMEM),
            pl.BlockSpec(memory_space=pltpu.VMEM),
        ],
        out_specs=pl.BlockSpec(memory_space=pltpu.VMEM),
        scratch_shapes=[
            pltpu.VMEM((count, height, width), gradients.dtype),
            pltpu.VMEM((count, height, width), gradients.dtype),
            pltpu.SemaphoreType.DMA((count,)),
            pltpu.SemaphoreType.DMA((count,)),
        ],
        compiler_params=pltpu.CompilerParams(
            collective_id=0, has_side_effects=True, vmem_limit_bytes=16 * 1024 * 1024
        ),
        name="collect_gradient",
    )(owners, gradients)


def spread_kernel(
    count,
    groups,
    owners_ref,
    u_ref,
    s_ref,
    out_ref,
    pieces,
    near,
    far,
    mine,
    piece_send,
    piece_recv,
    near_send,
    near_recv,
    far_send,
    far_recv,
):
    me, group = lax.axis_index("fsdp"), lax.axis_index("group")
    height = out_ref.shape[1]
    meet([("fsdp", count), ("group", groups)])
    near_copies, piece_copies, far_copies = [], [], []
    for d in range(1, count):
        to = lax.rem(me + d, count)
        near_copies.append(
            send(s_ref, near.at[me], near_send.at[d], near_recv.at[d], "fsdp", to)
        )
    for d in range(1, count):
        to = lax.rem(me + d, count)
        rows = pl.ds(pl.multiple_of(to * height, height), height)
        piece_copies.append(
            send(u_ref.at[rows], pieces.at[me], piece_send.at[d], piece_recv.at[d], "fsdp", to)
        )
    near[me] = s_ref[...]
    pieces[me] = u_ref[pl.ds(pl.multiple_of(me * height, height), height), :]
    for copy in near_copies:
        copy.wait()
    mine[...] = sum(near[f] for f in range(count))
    for d in range(1, groups):
        to = lax.rem(group + d, groups)
        far_copies.append(
            send(mine, far.at[group], far_send.at[d], far_recv.at[d], "group", to)
        )
    far[group] = mine[...]
    for copy in far_copies:
        copy.wait()
    total = jnp.sum(sum(far[g] for g in range(groups)), axis=1, keepdims=True)
    total = jnp.sum(total, axis=0, keepdims=True)
    entries = count * groups * u_ref.shape[0] * u_ref.shape[1]
    ceiling = clip_rms * entries**0.5
    scale = jnp.minimum(1.0, ceiling / jnp.sqrt(total + 1e-06))
    for copy in piece_copies:
        copy.wait()
    for j in range(count):
        piece = pieces[owners_ref[0, j]].astype(jnp.float32)
        out_ref[j] = (scale * piece).astype(out_ref.dtype)


def spread(owners, update, squares, count, groups):
    width = update.shape[1]
    height = update.shape[0] // count
    vmem = pl.BlockSpec(memory_space=pltpu.VMEM)
    semaphores = pltpu.SemaphoreType.DMA
    return pl.pallas_call(
        functools.partial(spread_kernel, count, groups),
        out_shape=jax.ShapeDtypeStruct((count, height, width), update.dtype),
        in_specs=[pl.BlockSpec(memory_space=pltpu.SMEM), vmem, vmem],
        out_specs=vmem,
        scratch_shapes=[
            pltpu.VMEM((count, height, width), update.dtype),
            pltpu.VMEM((count, 8, 128), jnp.float32),
            pltpu.VMEM((groups, 8, 128), jnp.float32),
            pltpu.VMEM((8, 128), jnp.float32),
            semaphores((count,)),
            semaphores((count,)),
            semaphores((count,)),
            semaphores((count,)),
            semaphores((groups,)),
            semaphores((groups,)),
        ],
        compiler_params=pltpu.CompilerParams(
            collective_id=1, has_side_effects=True, vmem_limit_bytes=16 * 1024 * 1024
        ),
        name="spread_update",
    )(owners, update, squares)


def on_device(gradients, owners, left_factors, right_factors, left_bases, right_bases, moments):
    count, groups = lax.axis_size("fsdp"), lax.axis_size("group")
    gradient = collect(owners, gradients, count)
    update, squares = local(
        gradient, left_factors, right_factors, left_bases, right_bases, moments
    )
    return spread(owners, update, squares, count, groups)


def solution(mesh):
    in_specs = (
        P("group", "fsdp", None),
        P("group", None),
        P(("fsdp", "group"), None, None),
        P(("fsdp", "group"), None, None),
        P(("fsdp", "group"), None, None),
        P(("fsdp", "group"), None, None),
        P(("fsdp", "group"), None, None),
    )
    out_specs = P("group", "fsdp", None)
    return jax.shard_map(
        on_device, mesh=mesh, in_specs=in_specs, out_specs=out_specs, check_vma=False
    )
```
